32 devices in a mesh: groups: 2 (over y), ta: 16 (over z, x, core).
Axes of the slice: x: 2, y: 2, z: 4, core: 2. Of those that a mesh axis runs over, the one named last changes fastest.
Arguments:
- sources: float32 [32, 2, 2, 2, 2, 96, 128], P(('groups', 'ta')), parts along dimension 0, may hold values from -6 to 6
- coarse_blocks: bfloat16 [32, 2, 2, 2, 2, 9, 128, 128], P(('groups', 'ta')), parts along dimension 0, may hold values from -0.5 to 0.5
Outputs:
- solution: float32 [32, 2, 2, 2, 2, 96, 128], P(('groups', 'ta')), parts along dimension 0
- residual: float32 [32, 2, 2, 2, 2, 96, 128], P(('groups', 'ta')), parts along dimension 0
The draws below stay inside these ranges and needn't reach their ends.
There are 2 independent parts, one for each index of `groups`. The reference program is written for one: setup_inputs(seed, part) draws one part's arguments, and reference() takes and returns one part's arrays. A program takes and returns all parts, laid end to end along the dimension named above; each array names one. Nothing has to cross between parts.
All inputs are finite; a program needn't handle non-finite values.
Results may differ from the reference program's by a relative error of at most 0.012.
Values may be sent and summed in bfloat16 or wider, within the bound.
A program may use at most 64 MiB of HBM per device.

```python
import jax
import jax.numpy as jnp
from jax import lax

NV = 128
LT = 2
LZ = 2
LY = 2
LX = 2
RHS = 96
CYCLES = 2
KRYLOV = 4
N_TA = 16


def shard_levels(stream_key, extent, cuts, least, top_value):
    def one(position, parts):
        steps = jax.random.uniform(jax.random.fold_in(jax.random.fold_in(stream_key, 6), position), (parts,), jnp.float32, least / len(cuts), top_value / len(cuts))
        return jnp.repeat(jnp.exp(steps), extent[position] // parts).reshape((-1,) + (1,) * (len(extent) - position - 1))

    level = one(*cuts[0])
    for cut in cuts[1:]:
        level = level * one(*cut)
    return level


def normal_values(own_key, dims, deviation, reach, split=(), held_as=jnp.bfloat16):
    factor_of = shard_levels(own_key, dims, split, -0.22, 0.18) if split else 1.0
    drawn = jax.random.normal(own_key, dims, jnp.float32) * deviation * factor_of
    return jnp.minimum(jnp.maximum(drawn, -reach), reach).astype(held_as)


def setup_inputs(seed: int = 0, part: int = 0) -> dict:
    key_list = jax.random.split(jax.random.key(seed), 3)
    own_keys = jax.random.split(jax.random.fold_in(key_list[2], part), 3)
    sources = normal_values(own_keys[0], (N_TA, LT, LZ, LY, LX, RHS, NV), 1.0, 6.0, ((0, 16),), jnp.float32)
    coarse_blocks = normal_values(own_keys[1], (N_TA, LT, LZ, LY, LX, 9, NV, NV), NV ** -0.5, 0.5, ((0, 16),))
    return {"sources": sources, "coarse_blocks": coarse_blocks}


mass_term = 3.5


def to_lattice(blocked):
    rest = blocked.shape[5:]
    count = blocked.shape[0] // 8
    grid = blocked.reshape((count, 2, 2, 2, LT, LZ, LY, LX) + rest)
    order = (0, 4, 1, 5, 2, 6, 3, 7) + tuple(range(8, 8 + len(rest)))
    return grid.transpose(order).reshape((count * LT, 2 * LZ, 2 * LY, 2 * LX) + rest)


def to_blocks(lattice):
    rest = lattice.shape[4:]
    count = lattice.shape[0] // LT
    grid = lattice.reshape((count, LT, 2, LZ, 2, LY, 2, LX) + rest)
    order = (0, 2, 4, 6, 1, 3, 5, 7) + tuple(range(8, 8 + len(rest)))
    return grid.transpose(order).reshape((count * 8, LT, LZ, LY, LX) + rest)


def operate(field, coarse_blocks):
    rounded = to_lattice(field.astype(jnp.bfloat16))
    neighbours = [rounded]
    for axis_index in (3, 2, 1, 0):
        neighbours.append(-jnp.roll(rounded, -1, axis_index))
        neighbours.append(-jnp.roll(rounded, 1, axis_index))
    stacked = to_blocks(jnp.stack(neighbours, axis=4))

    def one_block(pieces):
        stack_piece, block_piece = pieces
        return jnp.einsum('tzyxkri,tzyxkoi->tzyxro', stack_piece.astype(jnp.float32), block_piece.astype(jnp.float32))

    product = lax.map(one_block, (stacked, coarse_blocks))
    return mass_term * field + product


def dot_fields(first, second):
    return jnp.sum(first * second, axis=(0, 1, 2, 3, 4, 6))


def reference(sources, coarse_blocks):
    solution = jnp.zeros_like(sources)
    residual = sources
    for restart in range(CYCLES):
        directions = []
        images = []
        image_norms = []
        for step_index in range(KRYLOV):
            direction = residual
            image = operate(direction, coarse_blocks)
            heights = [dot_fields(earlier, image) for earlier in images]
            for earlier_index in range(step_index):
                factor = (heights[earlier_index] / image_norms[earlier_index])[:, None]
                image = image - factor * images[earlier_index]
                direction = direction - factor * directions[earlier_index]
            norm_now = dot_fields(image, image)
            alpha = (dot_fields(image, residual) / norm_now)[:, None]
            solution = solution + alpha * direction
            residual = residual - alpha * image
            directions.append(direction)
            images.append(image)
            image_norms.append(norm_now)
    return solution, residual
```

```python
import functools

import jax
import jax.numpy as jnp
from jax import lax
from jax.experimental import pallas as pl
from jax.experimental.pallas import tpu as pltpu
from jax.sharding import PartitionSpec as P

CYCLES = 2
KRYLOV = 4
PARTS = 2
UNROLL = 1

mass_term = 3.5
MESH = pl.DeviceIdType.MESH


def dot_t(left, right):
    return lax.dot_general(
        left, right, (((1,), (1,)), ((), ())), preferred_element_type=jnp.float32
    )


def kernel(
    n, src, blocks, sol, res, w, halo, dirs, imgs, sbuf, rbuf,
    halo_send, halo_recv, red_send, red_recv,
):
    sites, rhs, width = src.shape
    rows = rhs // PARTS
    half = sites // 2
    me = lax.axis_index("ta")
    group = lax.axis_index("groups")

    barrier = pltpu.get_barrier_semaphore()

    def peers(body):
        if n <= 16:
            for j in range(1, n):
                body(j)
        else:
            lax.fori_loop(1, n, lambda j, c: (body(j), c)[1], 0)

    def peer_at(j):
        return (group, lax.rem(me + j, n))

    peers(lambda j: pl.semaphore_signal(
        barrier, inc=1, device_id=peer_at(j), device_id_type=MESH))

    def flip(bit):
        step = 1 << bit
        return me + step - 2 * step * (lax.rem(me // step, 2))

    def halo_copies(p):
        ahead = lax.rem(me + 8, n)
        behind = lax.rem(me + n - 8, n)

        def one(src_ref, dst_ref, index, device):
            return pltpu.make_async_remote_copy(
                src_ref=src_ref, dst_ref=dst_ref,
                send_sem=halo_send.at[p, index], recv_sem=halo_recv.at[p, index],
                device_id=(group, device), device_id_type=MESH)

        copies = [
            one(w.at[p, pl.ds(half, half)], halo.at[3, p, pl.ds(half, half)], 3, ahead),
            one(w.at[p, pl.ds(0, half)], halo.at[3, p, pl.ds(0, half)], 4, behind),
        ]
        for bit in (2, 1, 0):
            copies.append(one(w.at[p], halo.at[bit, p], bit, flip(bit)))
        return copies

    def start_halo(p):
        for copy in halo_copies(p):
            copy.start()

    def rs(p):
        return pl.ds(p * rows, rows)

    eye = (lax.broadcasted_iota(jnp.int32, (rows, 128), 0)
           == lax.broadcasted_iota(jnp.int32, (rows, 128), 1))
    sub = lax.broadcasted_iota(jnp.int32, (8, 128), 0)

    def to_row(partial):
        column = jnp.sum(partial, axis=1, keepdims=True)
        return jnp.sum(jnp.where(eye, column, 0.0), axis=0, keepdims=True)

    def to_column(row):
        return jnp.sum(jnp.where(eye, row, 0.0), axis=1, keepdims=True)

    counter = [0]

    def reduce_start(partials):
        q = counter[0] % 2
        counter[0] += 1
        tile = jnp.zeros((8, 128), jnp.float32)
        for i, partial in enumerate(partials):
            tile = jnp.where(sub == i, to_row(partial), tile)
        sbuf[q] = tile

        def send(j):
            pltpu.make_async_remote_copy(
                src_ref=sbuf.at[q], dst_ref=rbuf.at[q, j - 1],
                send_sem=red_send.at[q], recv_sem=red_recv.at[q],
                device_id=peer_at(j), device_id_type=MESH).start()

        peers(send)
        return q, tile

    def reduce_end(handle):
        q, tile = handle
        pltpu.make_async_remote_copy(
            src_ref=rbuf.at[q], dst_ref=rbuf.at[q],
            send_sem=red_send.at[q], recv_sem=red_recv.at[q],
            device_id=peer_at(1), device_id_type=MESH).wait()
        return tile + jnp.sum(rbuf[q], axis=0)

    def over_sites(body, carry):
        def step(i, c):
            for q in range(UNROLL):
                c = body(i * UNROLL + q, i, q, c)
            return c
        return lax.fori_loop(0, sites // UNROLL, step, carry)

    def bit_of(i, q, bit):
        if (1 << bit) < UNROLL:
            return (q >> bit) & 1
        return lax.rem(i // ((1 << bit) // UNROLL), 2)

    def hop_terms(s, i, q, field_of, other):
        lefts, rights = [], []
        for bit in range(4):
            b = bit_of(i, q, bit)
            mate = s + (1 << bit) - 2 * (1 << bit) * b
            k = 2 + 2 * bit - b if other else 1 + 2 * bit + b
            lefts.append(field_of(bit, mate))
            rights.append(blocks[s, k])
        return dot_t(jnp.concatenate(lefts, axis=1), jnp.concatenate(rights, axis=1))

    def local_part(p, slot):
        def body(s, i, q, c):
            hops = hop_terms(s, i, q, lambda bit, m: w[p, m], False)
            own = dot_t(w[p, s], blocks[s, 0])
            imgs[slot, s, rs(p)] = mass_term * res[s, rs(p)] + own - hops
            return c
        over_sites(body, 0)

    zero = jnp.zeros((rows, width), jnp.float32)

    def process(p, k, norms, last):
        for copy in halo_copies(p):
            copy.wait_recv()

        def apply(s, i, q, c):
            hops = hop_terms(s, i, q, lambda bit, m: halo[bit, p, m], True)
            image = imgs[k, s, rs(p)] - hops
            imgs[k, s, rs(p)] = image
            if k == 0:
                return (c[0] + image * image, c[1] + image * res[s, rs(p)])
            return tuple(c[j] + image * imgs[j, s, rs(p)] for j in range(k))

        sums = over_sites(apply, (zero,) * (k if k else 2))
        if k:
            total = reduce_end(reduce_start(sums))
            factors = [to_column(total[j:j + 1] / norms[j]) for j in range(k)]

            def orthogonal(s, i, q, c):
                image = imgs[k, s, rs(p)]
                for j in range(k):
                    image = image - factors[j] * imgs[j, s, rs(p)]
                imgs[k, s, rs(p)] = image
                return (c[0] + image * image, c[1] + image * res[s, rs(p)])

            sums = over_sites(orthogonal, (zero, zero))
        handle = reduce_start(sums)

        def steer(s, i, q, c):
            direction = res[s, rs(p)]
            for j in range(k):
                direction = direction - factors[j] * dirs[j, s, rs(p)]
            dirs[k, s, rs(p)] = direction
            return c

        over_sites(steer, 0)
        for copy in halo_copies(p):
            copy.wait_send()
        total = reduce_end(handle)
        norm = total[0:1]
        alpha = to_column(total[1:2] / norm)

        def shrink(s, i, q, c):
            residual = res[s, rs(p)] - alpha * imgs[k, s, rs(p)]
            res[s, rs(p)] = residual
            w[p, s] = residual.astype(jnp.bfloat16)
            return c

        over_sites(shrink, 0)

        def advance(s, i, q, c):
            sol[s, rs(p)] = sol[s, rs(p)] + alpha * dirs[k, s, rs(p)]
            return c

        def go_on():
            start_halo(p)

        def prepare():
            local_part(p, (k + 1) % KRYLOV)

        if last is None:
            go_on()
            over_sites(advance, 0)
            prepare()
        else:
            pl.when(jnp.logical_not(last))(go_on)
            over_sites(advance, 0)
            pl.when(jnp.logical_not(last))(prepare)
        return norms + [norm]

    def fill(s, i, q, c):
        value = src[s]
        res[s] = value
        sol[s] = jnp.zeros_like(value)
        for p in range(PARTS):
            w[p, s] = value[p * rows:(p + 1) * rows].astype(jnp.bfloat16)
        return c

    over_sites(fill, 0)
    pl.semaphore_wait(barrier, n - 1)
    for p in range(PARTS):
        start_halo(p)
    for p in range(PARTS):
        local_part(p, 0)

    def cycle(index, c):
        norms = [[] for _ in range(PARTS)]
        for k in range(KRYLOV):
            for p in range(PARTS):
                last = index == CYCLES - 1 if k == KRYLOV - 1 else None
                norms[p] = process(p, k, norms[p], last)
        return c

    lax.fori_loop(0, CYCLES, cycle, 0)


def shards(sources, coarse_blocks):
    n = lax.axis_size("ta")
    shape = sources.shape
    rhs, width = shape[5], shape[6]
    sites = shape[1] * shape[2] * shape[3] * shape[4]
    count = coarse_blocks.shape[5]
    rows = rhs // PARTS
    field = jax.ShapeDtypeStruct((sites, rhs, width), jnp.float32)
    vmem = pl.BlockSpec(memory_space=pltpu.VMEM)
    solution, residual = pl.pallas_call(
        functools.partial(kernel, n),
        out_shape=(field, field),
        in_specs=[vmem, vmem],
        out_specs=(vmem, vmem),
        scratch_shapes=[
            pltpu.VMEM((PARTS, sites, rows, width), jnp.bfloat16),
            pltpu.VMEM((4, PARTS, sites, rows, width), jnp.bfloat16),
            pltpu.VMEM((KRYLOV, sites, rhs, width), jnp.float32),
            pltpu.VMEM((KRYLOV, sites, rhs, width), jnp.float32),
            pltpu.VMEM((2, 8, 128), jnp.float32),
            pltpu.VMEM((2, n - 1, 8, 128), jnp.float32),
            pltpu.SemaphoreType.DMA((PARTS, 5)),
            pltpu.SemaphoreType.DMA((PARTS, 5)),
            pltpu.SemaphoreType.DMA((2,)),
            pltpu.SemaphoreType.DMA((2,)),
        ],
        compiler_params=pltpu.CompilerParams(
            collective_id=0, has_side_effects=True, vmem_limit_bytes=40 << 20
        ),
    )(
        sources.reshape(sites, rhs, width),
        coarse_blocks.reshape(sites, count, width, width),
    )
    return solution.reshape(shape), residual.reshape(shape)


def solution(mesh):
    placed = (
        P(("groups", "ta"), None, None, None, None, None, None),
        P(("groups", "ta"), None, None, None, None, None, None, None),
    )
    return jax.shard_map(
        shards,
        mesh=mesh,
        in_specs=placed,
        out_specs=(
            P(("groups", "ta"), None, None, None, None, None, None),
            P(("groups", "ta"), None, None, None, None, None, None),
        ),
        check_vma=False,
    )
```

```python
import functools

import jax
import jax.numpy as jnp
from jax import lax
from jax.experimental import pallas as pl
from jax.experimental.pallas import tpu as pltpu
from jax.sharding import PartitionSpec as P

CYCLES = 2
KRYLOV = 4
PARTS = 2
SLOTS = 3
UNROLL = 1

mass_term = 3.5
MESH = pl.DeviceIdType.MESH


def dot(left, right):
    return lax.dot_general(
        left, right, (((1,), (0,)), ((), ())), preferred_element_type=jnp.float32
    )


def kernel(
    n, src, blocks_in, sol, res, blocks, w, halo, dirs, imgs, sbuf, rbuf,
    halo_send, halo_recv, red_send, red_recv,
):
    sites, rhs, width = src.shape
    rows = rhs // PARTS
    half = sites // 2
    me = lax.axis_index("ta")
    group = lax.axis_index("groups")

    barrier = pltpu.get_barrier_semaphore()

    def peers(body):
        if n <= 16:
            for j in range(1, n):
                body(j)
        else:
            lax.fori_loop(1, n, lambda j, c: (body(j), c)[1], 0)

    def peer_at(j):
        return (group, lax.rem(me + j, n))

    peers(lambda j: pl.semaphore_signal(
        barrier, inc=1, device_id=peer_at(j), device_id_type=MESH))

    def flip(bit):
        step = 1 << bit
        return me + step - 2 * step * (lax.rem(me // step, 2))

    def halo_copies(p):
        ahead = lax.rem(me + 8, n)
        behind = lax.rem(me + n - 8, n)

        def one(src_ref, dst_ref, index, device):
            return pltpu.make_async_remote_copy(
                src_ref=src_ref, dst_ref=dst_ref,
                send_sem=halo_send.at[p, index], recv_sem=halo_recv.at[p, index],
                device_id=(group, device), device_id_type=MESH)

        copies = [
            one(w.at[p, pl.ds(half, half)], halo.at[3, p, pl.ds(half, half)], 3, ahead),
            one(w.at[p, pl.ds(0, half)], halo.at[3, p, pl.ds(0, half)], 4, behind),
        ]
        for bit in (2, 1, 0):
            copies.append(one(w.at[p], halo.at[bit, p], bit, flip(bit)))
        return copies

    def start_halo(p):
        for copy in halo_copies(p):
            copy.start()

    def rs(p):
        return pl.ds(p * rows, rows)

    eye = (lax.broadcasted_iota(jnp.int32, (rows, 128), 0)
           == lax.broadcasted_iota(jnp.int32, (rows, 128), 1))
    sub = lax.broadcasted_iota(jnp.int32, (8, 128), 0)

    def to_row(partial):
        column = jnp.sum(partial, axis=1, keepdims=True)
        return jnp.sum(jnp.where(eye, column, 0.0), axis=0, keepdims=True)

    def to_column(row):
        return jnp.sum(jnp.where(eye, row, 0.0), axis=1, keepdims=True)

    def reduce_start(p, slot, partials):
        q = SLOTS * p + slot
        tile = jnp.zeros((8, 128), jnp.float32)
        for i, partial in enumerate(partials):
            tile = jnp.where(sub == i, to_row(partial), tile)
        sbuf[q] = tile

        def send(j):
            pltpu.make_async_remote_copy(
                src_ref=sbuf.at[q], dst_ref=rbuf.at[q, j - 1],
                send_sem=red_send.at[q], recv_sem=red_recv.at[q],
                device_id=peer_at(j), device_id_type=MESH).start()

        peers(send)
        return q, tile

    def reduce_end(handle):
        q, tile = handle
        pltpu.make_async_remote_copy(
            src_ref=rbuf.at[q], dst_ref=rbuf.at[q],
            send_sem=red_send.at[q], recv_sem=red_recv.at[q],
            device_id=peer_at(1), device_id_type=MESH).wait()
        return tile + jnp.sum(rbuf[q], axis=0)

    def over_sites(body, carry):
        def step(i, c):
            for q in range(UNROLL):
                c = body(i * UNROLL + q, i, q, c)
            return c
        return lax.fori_loop(0, sites // UNROLL, step, carry)

    def bit_of(i, q, bit):
        if (1 << bit) < UNROLL:
            return (q >> bit) & 1
        return lax.rem(i // ((1 << bit) // UNROLL), 2)

    def hop_terms(s, i, q, field_of, other):
        lefts, rights = [], []
        for bit in range(4):
            b = bit_of(i, q, bit)
            mate = s + (1 << bit) - 2 * (1 << bit) * b
            k = 2 + 2 * bit - b if other else 1 + 2 * bit + b
            lefts.append(field_of(bit, mate))
            rights.append(blocks[s, k])
        return dot(jnp.concatenate(lefts, axis=1), jnp.concatenate(rights, axis=0))

    def local_part(p, slot):
        def body(s, i, q, c):
            hops = hop_terms(s, i, q, lambda bit, m: w[p, m], False)
            own = dot(w[p, s], blocks[s, 0])
            imgs[slot, s, rs(p)] = mass_term * res[s, rs(p)] + own - hops
            return c
        over_sites(body, 0)

    zero = jnp.zeros((rows, width), jnp.float32)

    def process(k, norms, last):
        groups = range(PARTS)
        handles = [None] * PARTS
        factors = [[] for _ in groups]

        def apply(p, s, i, q, c):
            hops = hop_terms(s, i, q, lambda bit, m: halo[bit, p, m], True)
            image = imgs[k, s, rs(p)] - hops
            imgs[k, s, rs(p)] = image
            if k == 0:
                return (c[0] + image * image, c[1] + image * res[s, rs(p)])
            return tuple(c[j] + image * imgs[j, s, rs(p)] for j in range(k))

        def orthogonal(p, s, i, q, c):
            image = imgs[k, s, rs(p)]
            for j in range(k):
                image = image - factors[p][j] * imgs[j, s, rs(p)]
            imgs[k, s, rs(p)] = image
            return (c[0] + image * image, c[1] + image * res[s, rs(p)])

        def steer(p, s, i, q, c):
            direction = res[s, rs(p)]
            for j in range(k):
                direction = direction - factors[p][j] * dirs[j, s, rs(p)]
            dirs[k, s, rs(p)] = direction
            return c

        def shrink(p, alpha, s, i, q, c):
            residual = res[s, rs(p)] - alpha * imgs[k, s, rs(p)]
            res[s, rs(p)] = residual
            w[p, s] = residual.astype(jnp.bfloat16)
            return c

        def advance(p, alpha, s, i, q, c):
            sol[s, rs(p)] = sol[s, rs(p)] + alpha * dirs[k, s, rs(p)]
            return c

        def when_going_on(body):
            if last is None:
                body()
            else:
                pl.when(jnp.logical_not(last))(body)

        for p in groups:
            for copy in halo_copies(p):
                copy.wait_recv()
            sums = over_sites(functools.partial(apply, p), (zero,) * (k if k else 2))
            handles[p] = reduce_start(p, 0 if k else 2, sums)
        if k:
            for p in groups:
                total = reduce_end(handles[p])
                factors[p] = [to_column(total[j:j + 1] / norms[p][j]) for j in range(k)]
                sums = over_sites(functools.partial(orthogonal, p), (zero, zero))
                handles[p] = reduce_start(p, 1, sums)
        for p in groups:
            over_sites(functools.partial(steer, p), 0)
        for p in groups:
            for copy in halo_copies(p):
                copy.wait_send()
            total = reduce_end(handles[p])
            norm = total[0:1]
            norms[p].append(norm)
            alpha = to_column(total[1:2] / norm)
            over_sites(functools.partial(shrink, p, alpha), 0)
            when_going_on(lambda p=p: start_halo(p))
            over_sites(functools.partial(advance, p, alpha), 0)
        for p in groups:
            when_going_on(lambda p=p: local_part(p, (k + 1) % KRYLOV))

    def fill(s, i, q, c):
        value = src[s]
        res[s] = value
        sol[s] = jnp.zeros_like(value)
        for p in range(PARTS):
            w[p, s] = value[p * rows:(p + 1) * rows].astype(jnp.bfloat16)
        return c

    over_sites(fill, 0)
    pl.semaphore_wait(barrier, n - 1)
    for p in range(PARTS):
        start_halo(p)

    def turn(s, i, q, c):
        for k in range(blocks.shape[1]):
            blocks[s, k] = blocks_in[s, k].T
        return c

    over_sites(turn, 0)
    for p in range(PARTS):
        local_part(p, 0)

    def cycle(index, c):
        norms = [[] for _ in range(PARTS)]
        for k in range(KRYLOV):
            last = index == CYCLES - 1 if k == KRYLOV - 1 else None
            process(k, norms, last)
        return c

    lax.fori_loop(0, CYCLES, cycle, 0)


def shards(sources, coarse_blocks):
    n = lax.axis_size("ta")
    shape = sources.shape
    rhs, width = shape[5], shape[6]
    sites = shape[1] * shape[2] * shape[3] * shape[4]
    count = coarse_blocks.shape[5]
    rows = rhs // PARTS
    field = jax.ShapeDtypeStruct((sites, rhs, width), jnp.float32)
    vmem = pl.BlockSpec(memory_space=pltpu.VMEM)
    solution, residual = pl.pallas_call(
        functools.partial(kernel, n),
        out_shape=(field, field),
        in_specs=[vmem, vmem],
        out_specs=(vmem, vmem),
        scratch_shapes=[
            pltpu.VMEM((sites, count, width, width), jnp.bfloat16),
            pltpu.VMEM((PARTS, sites, rows, width), jnp.bfloat16),
            pltpu.VMEM((4, PARTS, sites, rows, width), jnp.bfloat16),
            pltpu.VMEM((KRYLOV, sites, rhs, width), jnp.float32),
            pltpu.VMEM((KRYLOV, sites, rhs, width), jnp.float32),
            pltpu.VMEM((SLOTS * PARTS, 8, 128), jnp.float32),
            pltpu.VMEM((SLOTS * PARTS, n - 1, 8, 128), jnp.float32),
            pltpu.SemaphoreType.DMA((PARTS, 5)),
            pltpu.SemaphoreType.DMA((PARTS, 5)),
            pltpu.SemaphoreType.DMA((SLOTS * PARTS,)),
            pltpu.SemaphoreType.DMA((SLOTS * PARTS,)),
        ],
        compiler_params=pltpu.CompilerParams(
            collective_id=0, has_side_effects=True, vmem_limit_bytes=40 << 20
        ),
    )(
        sources.reshape(sites, rhs, width),
        coarse_blocks.reshape(sites, count, width, width),
    )
    return solution.reshape(shape), residual.reshape(shape)


def solution(mesh):
    placed = (
        P(("groups", "ta"), None, None, None, None, None, None),
        P(("groups", "ta"), None, None, None, None, None, None, None),
    )
    return jax.shard_map(
        shards,
        mesh=mesh,
        in_specs=placed,
        out_specs=(
            P(("groups", "ta"), None, None, None, None, None, None),
            P(("groups", "ta"), None, None, None, None, None, None),
        ),
        check_vma=False,
    )
```

```python
import functools

import jax
import jax.numpy as jnp
from jax import lax
from jax.experimental import pallas as pl
from jax.experimental.pallas import tpu as pltpu
from jax.sharding import PartitionSpec as P

CYCLES = 2
KRYLOV = 4
PARTS = 2
SLOTS = 3
SLAB = 4
UNROLL = 1

mass_term = 3.5
MESH = pl.DeviceIdType.MESH


def dot(left, right):
    return lax.dot_general(
        left, right, (((1,), (0,)), ((), ())), preferred_element_type=jnp.float32
    )


def kernel(
    n, src, blocks_in, sol, res, blocks, w, halo, dirs, imgs, sbuf, rbuf,
    halo_send, halo_recv, red_send, red_recv,
):
    sites, rhs, width = src.shape
    rows = rhs // PARTS
    half = sites // 2
    me = lax.axis_index("ta")
    group = lax.axis_index("groups")

    barrier = pltpu.get_barrier_semaphore()

    def peers(body):
        if n <= 16:
            for j in range(1, n):
                body(j)
        else:
            lax.fori_loop(1, n, lambda j, c: (body(j), c)[1], 0)

    def peer_at(j):
        return (group, lax.rem(me + j, n))

    peers(lambda j: pl.semaphore_signal(
        barrier, inc=1, device_id=peer_at(j), device_id_type=MESH))

    def flip(bit):
        step = 1 << bit
        return me + step - 2 * step * (lax.rem(me // step, 2))

    def halo_copies(p):
        ahead = lax.rem(me + 8, n)
        behind = lax.rem(me + n - 8, n)

        def one(src_ref, dst_ref, index, device):
            return pltpu.make_async_remote_copy(
                src_ref=src_ref, dst_ref=dst_ref,
                send_sem=halo_send.at[p, index], recv_sem=halo_recv.at[p, index],
                device_id=(group, device), device_id_type=MESH)

        copies = [
            one(w.at[p, pl.ds(half, half)], halo.at[3, p, pl.ds(half, half)], 3, ahead),
            one(w.at[p, pl.ds(0, half)], halo.at[3, p, pl.ds(0, half)], 4, behind),
        ]
        for bit in (2, 1, 0):
            copies.append(one(w.at[p], halo.at[bit, p], bit, flip(bit)))
        return copies

    def start_halo(p):
        for copy in halo_copies(p):
            copy.start()

    def rs(p):
        return pl.ds(p * rows, rows)

    eye = (lax.broadcasted_iota(jnp.int32, (rows, 128), 0)
           == lax.broadcasted_iota(jnp.int32, (rows, 128), 1))
    sub = lax.broadcasted_iota(jnp.int32, (8, 128), 0)

    def to_row(partial):
        column = jnp.sum(partial, axis=1, keepdims=True)
        return jnp.sum(jnp.where(eye, column, 0.0), axis=0, keepdims=True)

    def to_column(row):
        return jnp.sum(jnp.where(eye, row, 0.0), axis=1, keepdims=True)

    def reduce_start(p, slot, partials):
        q = SLOTS * p + slot
        tile = jnp.zeros((8, 128), jnp.float32)
        for i, partial in enumerate(partials):
            tile = jnp.where(sub == i, to_row(partial), tile)
        sbuf[q] = tile

        def send(j):
            pltpu.make_async_remote_copy(
                src_ref=sbuf.at[q], dst_ref=rbuf.at[q, j - 1],
                send_sem=red_send.at[q], recv_sem=red_recv.at[q],
                device_id=peer_at(j), device_id_type=MESH).start()

        peers(send)
        return q, tile

    def reduce_end(handle):
        q, tile = handle
        pltpu.make_async_remote_copy(
            src_ref=rbuf.at[q], dst_ref=rbuf.at[q],
            send_sem=red_send.at[q], recv_sem=red_recv.at[q],
            device_id=peer_at(1), device_id_type=MESH).wait()
        return tile + jnp.sum(rbuf[q], axis=0)

    def over_sites(body, carry):
        def step(i, c):
            for q in range(UNROLL):
                c = body(i * UNROLL + q, i, q, c)
            return c
        return lax.fori_loop(0, sites // UNROLL, step, carry)

    def over_slabs(body, carry):
        def step(i, c):
            return body(pl.ds(i * SLAB, SLAB), i, 0, c)
        return lax.fori_loop(0, sites // SLAB, step, carry)

    def bit_of(i, q, bit):
        if (1 << bit) < UNROLL:
            return (q >> bit) & 1
        return lax.rem(i // ((1 << bit) // UNROLL), 2)

    def hop_terms(s, i, q, field_of, other):
        lefts, rights = [], []
        for bit in range(4):
            b = bit_of(i, q, bit)
            mate = s + (1 << bit) - 2 * (1 << bit) * b
            k = 2 + 2 * bit - b if other else 1 + 2 * bit + b
            lefts.append(field_of(bit, mate))
            rights.append(blocks[s, k])
        return dot(jnp.concatenate(lefts, axis=1), jnp.concatenate(rights, axis=0))

    def local_part(p, slot):
        def body(s, i, q, c):
            hops = hop_terms(s, i, q, lambda bit, m: w[p, m], False)
            own = dot(w[p, s], blocks[s, 0])
            imgs[slot, s, rs(p)] = mass_term * res[s, rs(p)] + own - hops
            return c
        over_sites(body, 0)

    zero = jnp.zeros((rows, width), jnp.float32)

    def process(k, norms, last):
        groups = range(PARTS)
        handles = [None] * PARTS
        factors = [[] for _ in groups]

        def apply(p, s, i, q, c):
            hops = hop_terms(s, i, q, lambda bit, m: halo[bit, p, m], True)
            image = imgs[k, s, rs(p)] - hops
            imgs[k, s, rs(p)] = image
            if k == 0:
                return (c[0] + image * image, c[1] + image * res[s, rs(p)])
            return tuple(c[j] + image * imgs[j, s, rs(p)] for j in range(k))

        def orthogonal(p, s, i, q, c):
            image = imgs[k, s, rs(p)]
            for j in range(k):
                image = image - factors[p][j] * imgs[j, s, rs(p)]
            imgs[k, s, rs(p)] = image
            toward = image * res[s, rs(p)]
            return (c[0] + jnp.sum(image * image, axis=0), c[1] + jnp.sum(toward, axis=0))

        def steer(p, s, i, q, c):
            direction = res[s, rs(p)]
            for j in range(k):
                direction = direction - factors[p][j] * dirs[j, s, rs(p)]
            dirs[k, s, rs(p)] = direction
            return c

        def shrink(p, alpha, s, i, q, c):
            residual = res[s, rs(p)] - alpha * imgs[k, s, rs(p)]
            res[s, rs(p)] = residual
            w[p, s] = residual.astype(jnp.bfloat16)
            return c

        def advance(p, alpha, s, i, q, c):
            sol[s, rs(p)] = sol[s, rs(p)] + alpha * dirs[k, s, rs(p)]
            return c

        def when_going_on(body):
            if last is None:
                body()
            else:
                pl.when(jnp.logical_not(last))(body)

        for p in groups:
            for copy in halo_copies(p):
                copy.wait_recv()
            sums = over_sites(functools.partial(apply, p), (zero,) * (k if k else 2))
            handles[p] = reduce_start(p, 0 if k else 2, sums)
        if k:
            for p in groups:
                total = reduce_end(handles[p])
                factors[p] = [to_column(total[j:j + 1] / norms[p][j]) for j in range(k)]
                sums = over_slabs(functools.partial(orthogonal, p), (zero, zero))
                handles[p] = reduce_start(p, 1, sums)
        for p in groups:
            over_slabs(functools.partial(steer, p), 0)
        for p in groups:
            for copy in halo_copies(p):
                copy.wait_send()
            total = reduce_end(handles[p])
            norm = total[0:1]
            norms[p].append(norm)
            alpha = to_column(total[1:2] / norm)
            over_slabs(functools.partial(shrink, p, alpha), 0)
            when_going_on(lambda p=p: start_halo(p))
            over_slabs(functools.partial(advance, p, alpha), 0)
        for p in groups:
            when_going_on(lambda p=p: local_part(p, (k + 1) % KRYLOV))

    def fill(s, i, q, c):
        value = src[s]
        res[s] = value
        sol[s] = jnp.zeros_like(value)
        for p in range(PARTS):
            w[p, s] = value[p * rows:(p + 1) * rows].astype(jnp.bfloat16)
        return c

    over_sites(fill, 0)
    pl.semaphore_wait(barrier, n - 1)
    for p in range(PARTS):
        start_halo(p)

    def turn(s, i, q, c):
        for k in range(blocks.shape[1]):
            blocks[s, k] = blocks_in[s, k].T
        return c

    over_sites(turn, 0)
    for p in range(PARTS):
        local_part(p, 0)

    def cycle(index, c):
        norms = [[] for _ in range(PARTS)]
        for k in range(KRYLOV):
            last = index == CYCLES - 1 if k == KRYLOV - 1 else None
            process(k, norms, last)
        return c

    lax.fori_loop(0, CYCLES, cycle, 0)


def shards(sources, coarse_blocks):
    n = lax.axis_size("ta")
    shape = sources.shape
    rhs, width = shape[5], shape[6]
    sites = shape[1] * shape[2] * shape[3] * shape[4]
    count = coarse_blocks.shape[5]
    rows = rhs // PARTS
    field = jax.ShapeDtypeStruct((sites, rhs, width), jnp.float32)
    vmem = pl.BlockSpec(memory_space=pltpu.VMEM)
    solution, residual = pl.pallas_call(
        functools.partial(kernel, n),
        out_shape=(field, field),
        in_specs=[vmem, vmem],
        out_specs=(vmem, vmem),
        scratch_shapes=[
            pltpu.VMEM((sites, count, width, width), jnp.bfloat16),
            pltpu.VMEM((PARTS, sites, rows, width), jnp.bfloat16),
            pltpu.VMEM((4, PARTS, sites, rows, width), jnp.bfloat16),
            pltpu.VMEM((KRYLOV, sites, rhs, width), jnp.float32),
            pltpu.VMEM((KRYLOV, sites, rhs, width), jnp.float32),
            pltpu.VMEM((SLOTS * PARTS, 8, 128), jnp.float32),
            pltpu.VMEM((SLOTS * PARTS, n - 1, 8, 128), jnp.float32),
            pltpu.SemaphoreType.DMA((PARTS, 5)),
            pltpu.SemaphoreType.DMA((PARTS, 5)),
            pltpu.SemaphoreType.DMA((SLOTS * PARTS,)),
            pltpu.SemaphoreType.DMA((SLOTS * PARTS,)),
        ],
        compiler_params=pltpu.CompilerParams(
            collective_id=0, has_side_effects=True, vmem_limit_bytes=40 << 20
        ),
    )(
        sources.reshape(sites, rhs, width),
        coarse_blocks.reshape(sites, count, width, width),
    )
    return solution.reshape(shape), residual.reshape(shape)


def solution(mesh):
    placed = (
        P(("groups", "ta"), None, None, None, None, None, None),
        P(("groups", "ta"), None, None, None, None, None, None, None),
    )
    return jax.shard_map(
        shards,
        mesh=mesh,
        in_specs=placed,
        out_specs=(
            P(("groups", "ta"), None, None, None, None, None, None),
            P(("groups", "ta"), None, None, None, None, None, None),
        ),
        check_vma=False,
    )
```
